128 devices in a mesh: seq: 8 (over z, core), head: 16 (over y, x).
Axes of the slice: x: 4, y: 4, z: 4, core: 2. Of those that a mesh axis runs over, the one named last changes fastest.
Arguments:
- queries: bfloat16 [16384, 2048], P(('seq', 'head')), may hold values from -6 to 6
- key_rows: bfloat16 [16384, 2048], P(('seq', 'head')), may hold values from -6 to 6
- value_rows: bfloat16 [16384, 2048], P(('seq', 'head')), may hold values from -6 to 6
- ridge_diag: float32 [16, 128], replicated, may hold values from 0.5 to 4
Outputs:
- mixed: bfloat16 [16384, 2048], P(('seq', 'head'))
The draws below stay inside these ranges and needn't reach their ends.
All inputs are finite; a program needn't handle non-finite values.
Results may differ from the reference program's by a relative error of at most 0.0075.
The reference program's roundings to bfloat16 on the way (of `q_unit` and `k_unit`) count: a program that leaves them out, or rounds other values in their place, can miss the bound.
Values may be sent and summed in bfloat16 or wider, within the bound.
No kernel may reach another device: no remote copies, remote signals or barrier semaphores. Data moves between devices by JAX's collectives and lax.ppermute only.
A program may use at most 64 MiB of HBM per device.

```python
import math
import jax
import jax.numpy as jnp
from jax import lax

HEADS = 16
DK = 128
GROUP = 64
TOK_DEV = 128
TOKENS = 16384


def draw_key_rows(key, part):
    rank_count = max(DK // 8, 2)
    switch_len = 16 * GROUP
    segment_count = TOKENS // switch_len + 2
    shift_key = jax.random.fold_in(key, 11)
    basis_key = jax.random.fold_in(key, 12)
    coeff_key = jax.random.fold_in(key, 13)
    noise_key = jax.random.fold_in(key, 14)
    shift_by = jax.random.randint(shift_key, (HEADS,), 0, switch_len, dtype=jnp.int32)
    positions = jnp.arange(TOKENS, dtype=jnp.int32)
    segment = (positions[:, None] + shift_by[None, :]) // switch_len
    basis = jax.random.normal(basis_key, (rank_count, HEADS, segment_count, DK), jnp.float32)
    coeffs = jax.random.normal(coeff_key, (TOKENS, HEADS, rank_count), jnp.float32)
    noise = 0.05 * jax.random.normal(noise_key, (TOKENS, HEADS, DK), jnp.float32)
    grade = jnp.exp(-jnp.log(10.0) * jnp.arange(rank_count, dtype=jnp.float32) / (rank_count - 1))
    head_index = jnp.arange(HEADS, dtype=jnp.int32)[None, :]
    total = noise
    for which in range(rank_count):
        picked = basis[which][head_index, segment]
        total = total + (coeffs[:, :, which] * grade[which])[:, :, None] * picked
    return jnp.clip(total, -6.0, 6.0).reshape(TOKENS, HEADS * DK).astype(jnp.bfloat16)


def shard_levels(own_key, extent, pieces, low, largest):
    factor_of, own = 1.0, jax.random.fold_in(own_key, 6)
    for dim, parts in pieces:
        steps = jnp.exp(jax.random.uniform(jax.random.fold_in(own, dim), (parts,), jnp.float32, low / len(pieces), largest / len(pieces)))
        factor_of = factor_of * jnp.repeat(steps, extent[dim] // parts).reshape([-1 if axis == dim else 1 for axis in range(len(extent))])
    return factor_of


def gaussian(key, shape, deviation, most, cuts=(), kind=jnp.bfloat16):
    entries = deviation * jax.random.normal(key, shape, jnp.float32)
    if cuts:
        entries = entries * shard_levels(key, shape, cuts, -0.22, 0.18)
    return jnp.clip(entries, -most, most).astype(kind)


def setup_inputs(seed: int = 0) -> dict:
    seeds = jax.random.split(jax.random.key(seed), 5)
    queries = gaussian(seeds[0], (TOKENS, HEADS * DK), 1.0, 6.0, ((0, 128),))
    key_rows = draw_key_rows(jax.random.fold_in(seeds[4], 71), 0)
    value_rows = gaussian(seeds[2], (TOKENS, HEADS * DK), 1.0, 6.0, ((0, 128),))
    ridge_diag = jnp.clip(jnp.exp(jax.random.uniform(seeds[3], (HEADS, DK), jnp.float32, math.log(0.5), math.log(4.0))), 0.5, 4.0)
    return dict(queries=queries, key_rows=key_rows, value_rows=value_rows, ridge_diag=ridge_diag)


epsilon = 1e-06
highest = lax.Precision.HIGHEST

def unit_rows(matrix):
    values_f = matrix.astype(jnp.float32)
    scale_back = lax.rsqrt(lax.optimization_barrier(jnp.sum(values_f * values_f, axis=-1, keepdims=True)) + epsilon)
    return (values_f * scale_back).astype(jnp.bfloat16)

def reference(queries, key_rows, value_rows, ridge_diag):
    per_block = TOK_DEV // GROUP
    block_count = TOKENS // TOK_DEV

    def head_out(head_index):
        offset = head_index * DK
        q_head = lax.dynamic_slice_in_dim(queries, offset, DK, 1)
        k_head = lax.dynamic_slice_in_dim(key_rows, offset, DK, 1)
        v_head = lax.dynamic_slice_in_dim(value_rows, offset, DK, 1)
        ridge_here = lax.dynamic_slice_in_dim(ridge_diag, head_index, 1, 0)[0]
        q_unit = unit_rows(q_head).reshape(block_count, per_block, GROUP, DK)
        k_unit = unit_rows(k_head).reshape(block_count, per_block, GROUP, DK)
        v_block = v_head.reshape(block_count, per_block, GROUP, DK)

        def advance(running, inputs_now):
            gram_run, vk_run = running
            q_now, k_now, v_now = inputs_now
            k_f = k_now.astype(jnp.float32)
            v_f = v_now.astype(jnp.float32)
            group_gram = jnp.einsum('cti,ctj->cij', k_f, k_f, precision=highest)
            group_vk = jnp.einsum('ctv,ctk->cvk', v_f, k_f, precision=highest)
            gram_inc = jnp.cumsum(group_gram, axis=0)
            vk_inc = jnp.cumsum(group_vk, axis=0)
            gram_start = gram_run + gram_inc - group_gram
            vk_start = vk_run + vk_inc - group_vk
            system = gram_start + jnp.diag(ridge_here)
            factor = jnp.linalg.cholesky(system)
            targets = jnp.swapaxes(q_now.astype(jnp.float32), -1, -2)
            half_solved = jax.scipy.linalg.solve_triangular(factor, targets, lower=True)
            solved = jax.scipy.linalg.solve_triangular(factor, half_solved, lower=True, trans=1)
            carried = jnp.einsum('cvk,ckt->ctv', vk_start, solved, precision=highest)
            scores = jnp.einsum('csk,ckt->cts', k_f, solved, precision=highest)
            causal = jnp.arange(GROUP)[None, :] <= jnp.arange(GROUP)[:, None]
            within = jnp.einsum('cts,csv->ctv', jnp.where(causal[None], scores, 0.0), v_f, precision=highest)
            result = (carried + within).astype(jnp.bfloat16)
            return ((gram_run + gram_inc[-1], vk_run + vk_inc[-1]), result)
        zero_state = jnp.zeros((DK, DK), jnp.float32)
        _, outputs = lax.scan(advance, (zero_state, zero_state), (q_unit, k_unit, v_block))
        return outputs.reshape(TOKENS, DK)
    stacked = lax.map(head_out, jnp.arange(HEADS, dtype=jnp.int32))
    return jnp.transpose(stacked, (1, 0, 2)).reshape(TOKENS, HEADS * DK)
```

```python
import jax
import jax.numpy as jnp
from jax import lax
from jax.experimental import pallas as pl
from jax.experimental.pallas import tpu as pltpu
from jax.sharding import PartitionSpec as P

HEADS = 16
DK = 128
GROUP = 64
ROWS = 128
SOURCES = 16
GROUPS = SOURCES * ROWS // GROUP
EDGE = 32
LEVELS = DK // EDGE
PACK = DK // EDGE

f32, bf16 = jnp.float32, jnp.bfloat16
epsilon = 1e-06


def lanes(shape):
    return lax.broadcasted_iota(jnp.int32, shape, len(shape) - 1)


def unit_rows(values):
    values_f = values.astype(f32)
    scale_back = lax.rsqrt(jnp.sum(values_f * values_f, axis=-1, keepdims=True) + epsilon)
    return (values_f * scale_back).astype(bf16)


def unit_kernel(q_ref, k_ref, v_ref, out_ref):
    for h in range(HEADS):
        columns = slice(h * DK, (h + 1) * DK)
        out_ref[h, :ROWS, :] = unit_rows(q_ref[:, columns])
        out_ref[h, ROWS : 2 * ROWS, :] = unit_rows(k_ref[:, columns])
        out_ref[h, 2 * ROWS :, :] = v_ref[:, columns]


def total_kernel(qkv_ref, out_ref):
    def add(source, total):
        k = qkv_ref[source, ROWS : 2 * ROWS, :]
        v = qkv_ref[source, 2 * ROWS :, :]
        return total + turned_dot(k, jnp.concatenate([k, v], axis=1))

    out_ref[...] = lax.fori_loop(0, SOURCES, add, jnp.zeros((DK, 2 * DK), f32), unroll=True)


def turned_dot(left, right):
    return lax.dot_general(left, right, (((0,), (0,)), ((), ())), preferred_element_type=f32)


def dot(left, right):
    return jnp.dot(left, right, preferred_element_type=f32)


def spread(x, quarter):
    x = jnp.where(lanes(x.shape) // EDGE == quarter, x, 0.0)
    x = x + pltpu.roll(x, EDGE, 1)
    return x + pltpu.roll(x, 2 * EDGE, 1)


def left_parts(x):
    lane = lanes(x.shape)
    rest = x - x.astype(bf16).astype(f32)
    low = rest - rest.astype(bf16).astype(f32)
    first = jnp.where(lane < 3 * EDGE, x, rest).astype(bf16)
    second = jnp.where(lane < 2 * EDGE, rest, low).astype(bf16)
    return jnp.concatenate([first, second], axis=1)


def right_parts(x):
    high = x.astype(bf16)
    rest = x - high.astype(f32)
    middle = rest.astype(bf16)
    low = (rest - middle.astype(f32)).astype(bf16)
    return jnp.concatenate([high, middle, low, high, middle, low, high, middle], axis=0)


def two_parts(x):
    high = x.astype(bf16)
    return high, (x - high.astype(f32)).astype(bf16)


def invert(rows):
    lane = lanes((8, DK)) % EDGE
    base = lanes((8, DK)) - lane
    for j in range(EDGE):
        here = lane == j

        def pick(x):
            return jnp.take_along_axis(x, base + j, axis=1)

        inverse = 1.0 / pick(rows[j])
        pivot = jnp.where(here, inverse, rows[j] * inverse)
        for r in range(EDGE):
            if r != j:
                rows[r] = jnp.where(here, 0.0, rows[r]) - pick(rows[r]) * pivot
        rows[j] = pivot
    return rows


def solve_kernel(mine_ref, qkv_ref, totals_ref, ridge_ref, out_ref, work, vk_start, running, packed):
    mine = mine_ref[0]
    row = lax.broadcasted_iota(jnp.int32, (DK, DK), 0)
    diagonal = jnp.where(row == lanes((DK, DK)), jnp.broadcast_to(ridge_ref[...], (DK, DK)), 0.0)
    start = jnp.concatenate([diagonal, jnp.zeros((DK, DK), f32)], axis=1)
    for i in range(totals_ref.shape[0] - 1):
        start = start + jnp.where(i < mine, 1.0, 0.0) * totals_ref[i]
    running[...] = start

    def fill(source, _):
        for half in range(ROWS // GROUP):
            c = source * (ROWS // GROUP) + half
            now = running[...]
            first = half * GROUP
            q = qkv_ref[source, first : first + GROUP, :]
            k = qkv_ref[source, ROWS + first : ROWS + first + GROUP, :]
            v = qkv_ref[source, 2 * ROWS + first : 2 * ROWS + first + GROUP, :]
            work[c, :DK, :] = now[:, :DK]
            work[c, DK:, :] = q.astype(f32)
            vk_start[c] = now[:, DK:]
            running[...] = now + turned_dot(k, jnp.concatenate([k, v], axis=1))
        return 0

    lax.fori_loop(0, SOURCES, fill, 0)

    for level in range(LEVELS):
        at = level * EDGE

        for s in range(GROUPS // PACK):
            tile = None
            for part in range(PACK):
                block = work[s * PACK + part, at : at + EDGE, :]
                if part != level:
                    block = pltpu.roll(block, (EDGE * (part - level)) % DK, 1)
                tile = block if part == 0 else jnp.where(lanes(block.shape) // EDGE == part, block, tile)
            packed[pl.ds(s, EDGE, stride=8), :] = tile
        rows = invert([packed[8 * r : 8 * r + 8, :] for r in range(EDGE)])
        for r in range(EDGE):
            packed[8 * r : 8 * r + 8, :] = rows[r]

        first = at + EDGE

        def eliminate(s, _):
            tile = packed[pl.ds(s, EDGE, stride=8), :]
            for part in range(PACK):
                c = s * PACK + part
                inverse = spread(tile, part)
                panel = dot(left_parts(inverse), right_parts(work[c, at:first, :]))
                panel = jnp.where(lanes(panel.shape) // EDGE == level, -inverse, panel)
                below = work[c, first:, :]
                change = dot(left_parts(spread(below, level)), right_parts(panel))
                work[c, first:, :] = jnp.where(lanes(below.shape) // EDGE == level, 0.0, below) - change
            return 0

        lax.fori_loop(0, GROUPS // PACK, eliminate, 0)

    def apply(source, _):
        for half in range(ROWS // GROUP):
            c = source * (ROWS // GROUP) + half
            first = half * GROUP
            k = qkv_ref[source, ROWS + first : ROWS + first + GROUP, :]
            v = qkv_ref[source, 2 * ROWS + first : 2 * ROWS + first + GROUP, :]
            high, low = two_parts(work[c, DK:, :])
            vk_high, vk_low = two_parts(vk_start[c])
            mixed = dot(jnp.concatenate([high, high], axis=1), jnp.concatenate([vk_high, vk_low], axis=0))
            mixed = mixed + dot(low, vk_high)
            scores = lax.dot_general(
                jnp.concatenate([high, low], axis=1),
                jnp.concatenate([k, k], axis=1),
                (((1,), (1,)), ((), ())),
                preferred_element_type=f32,
            )
            causal = lanes((GROUP, GROUP)) <= lax.broadcasted_iota(jnp.int32, (GROUP, GROUP), 0)
            high, low = two_parts(jnp.where(causal, scores, 0.0))
            mixed = mixed + dot(high, v) + dot(low, v)
            out_ref[source, first : first + GROUP, :] = mixed.astype(bf16)
        return 0

    lax.fori_loop(0, SOURCES, apply, 0)


def whole():
    return pl.BlockSpec(memory_space=pltpu.VMEM)


def body(queries, key_rows, value_rows, ridge_diag):
    parts = pl.pallas_call(
        unit_kernel,
        out_shape=jax.ShapeDtypeStruct((HEADS, 3 * ROWS, DK), bf16),
        in_specs=[whole()] * 3,
        out_specs=whole(),
        name="unit",
    )(queries, key_rows, value_rows)
    parts = lax.all_to_all(parts, "head", split_axis=0, concat_axis=0, tiled=True)
    total = pl.pallas_call(
        total_kernel,
        out_shape=jax.ShapeDtypeStruct((DK, 2 * DK), f32),
        in_specs=[whole()],
        out_specs=whole(),
        name="total",
    )(parts)
    totals = lax.all_gather(total, "seq")
    ridge_here = lax.dynamic_slice_in_dim(ridge_diag, lax.axis_index("head"), 1, 0)
    mine = lax.axis_index("seq").astype(jnp.int32).reshape(1)
    mixed = pl.pallas_call(
        solve_kernel,
        out_shape=jax.ShapeDtypeStruct((SOURCES, ROWS, DK), bf16),
        in_specs=[pl.BlockSpec(memory_space=pltpu.SMEM)] + [whole()] * 3,
        out_specs=whole(),
        scratch_shapes=[
            pltpu.VMEM((GROUPS, DK + GROUP, DK), f32),
            pltpu.VMEM((GROUPS, DK, DK), f32),
            pltpu.VMEM((DK, 2 * DK), f32),
            pltpu.VMEM((EDGE * 8, DK), f32),
        ],
        compiler_params=pltpu.CompilerParams(vmem_limit_bytes=40 * 2**20),
        name="solve",
    )(mine, parts, totals, ridge_here)
    mixed = lax.all_to_all(mixed, "head", split_axis=0, concat_axis=0, tiled=True)
    return jnp.transpose(mixed, (1, 0, 2)).reshape(ROWS, HEADS * DK)


def solution(mesh):
    in_specs = (P(("seq", "head"), None), P(("seq", "head"), None), P(("seq", "head"), None), P())
    out_specs = P(("seq", "head"), None)
    return jax.shard_map(body, mesh=mesh, in_specs=in_specs, out_specs=out_specs, check_vma=False)
```

```python
import jax
import jax.numpy as jnp
from jax import lax
from jax.experimental import pallas as pl
from jax.experimental.pallas import tpu as pltpu
from jax.sharding import PartitionSpec as P

HEADS = 16
DK = 128
GROUP = 64
ROWS = 128
SOURCES = 16
GROUPS = SOURCES * ROWS // GROUP
EDGE = 32
LEVELS = DK // EDGE
PACK = DK // EDGE

f32, bf16 = jnp.float32, jnp.bfloat16
epsilon = 1e-06


def lanes(shape):
    return lax.broadcasted_iota(jnp.int32, shape, len(shape) - 1)


def unit_rows(values):
    values_f = values.astype(f32)
    scale_back = lax.rsqrt(jnp.sum(values_f * values_f, axis=-1, keepdims=True) + epsilon)
    return (values_f * scale_back).astype(bf16)


def unit_kv_kernel(k_ref, v_ref, out_ref):
    for h in range(HEADS):
        columns = slice(h * DK, (h + 1) * DK)
        out_ref[h, :ROWS, :] = unit_rows(k_ref[:, columns])
        out_ref[h, ROWS:, :] = v_ref[:, columns]


def unit_q_kernel(q_ref, out_ref):
    for h in range(HEADS):
        out_ref[h] = unit_rows(q_ref[:, h * DK : (h + 1) * DK])


def total_kernel(kv_ref, out_ref):
    def add(source, total):
        k = kv_ref[source, :ROWS, :]
        v = kv_ref[source, ROWS:, :]
        return total + turned_dot(k, jnp.concatenate([k, v], axis=1))

    out_ref[...] = lax.fori_loop(0, SOURCES, add, jnp.zeros((DK, 2 * DK), f32), unroll=True)


def token_kernel(mixed_ref, out_ref):
    for h in range(HEADS):
        out_ref[:, h * DK : (h + 1) * DK] = mixed_ref[h]


def turned_dot(left, right):
    return lax.dot_general(left, right, (((0,), (0,)), ((), ())), preferred_element_type=f32)


def dot(left, right):
    return jnp.dot(left, right, preferred_element_type=f32)


def spread(x, quarter):
    return jnp.take_along_axis(x, quarter * EDGE + lanes(x.shape) % EDGE, axis=1)


def left_parts(x):
    lane = lanes(x.shape)
    rest = x - x.astype(bf16).astype(f32)
    low = rest - rest.astype(bf16).astype(f32)
    first = jnp.where(lane < 3 * EDGE, x, rest).astype(bf16)
    second = jnp.where(lane < 2 * EDGE, rest, low).astype(bf16)
    return jnp.concatenate([first, second], axis=1)


def right_parts(x):
    high = x.astype(bf16)
    rest = x - high.astype(f32)
    middle = rest.astype(bf16)
    low = (rest - middle.astype(f32)).astype(bf16)
    return jnp.concatenate([high, middle, low, high, middle, low, high, middle], axis=0)


def two_parts(x):
    high = x.astype(bf16)
    return high, (x - high.astype(f32)).astype(bf16)


def invert(rows):
    lane = lanes((8, DK)) % EDGE
    base = lanes((8, DK)) - lane

    def pick(x, j):
        return jnp.take_along_axis(x, base + j, axis=1)

    for j in range(0, EDGE, 2):
        first, second = rows[j], rows[j + 1]
        a, b, d = pick(first, j), pick(first, j + 1), pick(second, j + 1)
        scale = 1.0 / (a * d - b * b)
        a, b, d = a * scale, b * scale, d * scale
        at_first, at_second = lane == j, lane == j + 1
        pivot_first = jnp.where(at_first, d, jnp.where(at_second, -b, d * first - b * second))
        pivot_second = jnp.where(at_first, -b, jnp.where(at_second, a, a * second - b * first))
        for r in [*range(j + 2, EDGE), *range(j)]:
            x = rows[r]
            kept = jnp.where(at_first | at_second, 0.0, x)
            rows[r] = kept - pick(x, j) * pivot_first - pick(x, j + 1) * pivot_second
        rows[j], rows[j + 1] = pivot_first, pivot_second
    return rows


def solve_kernel(odd_ref, q_ref, kv_ref, one_ref, two_ref, three_ref, partner_ref, ridge_ref, out_ref, work_even, work_odd, vk_start, packed):
    row = lax.broadcasted_iota(jnp.int32, (DK, DK), 0)
    diagonal = jnp.where(row == lanes((DK, DK)), jnp.broadcast_to(ridge_ref[...], (DK, DK)), 0.0)
    start = one_ref[...] + two_ref[...] + three_ref[...]
    start = start + jnp.where(odd_ref[0] == 1, partner_ref[...], 0.0)
    work_even[0, :DK, :] = start[:, :DK] + diagonal
    vk_start[0] = start[:, DK:]

    def fill(source, _):
        for half in range(ROWS // GROUP):
            c = source * (ROWS // GROUP) + half
            first = half * GROUP
            k = kv_ref[source, first : first + GROUP, :]
            v = kv_ref[source, ROWS + first : ROWS + first + GROUP, :]
            work_even[c, DK:, :] = q_ref[source, first : first + GROUP, :].astype(f32)
            group = turned_dot(k, jnp.concatenate([k, v], axis=1))
            work_even[c + 1, :DK, :] = work_even[c, :DK, :] + group[:, :DK]
            vk_start[c + 1] = vk_start[c] + group[:, DK:]
        return 0

    lax.fori_loop(0, SOURCES, fill, 0, unroll=2)

    work = (work_even, work_odd)
    for level in range(LEVELS):
        before, after = work[level % 2], work[1 - level % 2]
        at = level * EDGE
        first = at + EDGE

        for s in range(GROUPS // PACK):
            tile = None
            for part in range(PACK):
                block = before[s * PACK + part, at:first, :]
                if part != level:
                    block = pltpu.roll(block, (EDGE * (part - level)) % DK, 1)
                tile = block if part == 0 else jnp.where(lanes(block.shape) // EDGE == part, block, tile)
            packed[pl.ds(s, EDGE, stride=8), :] = tile
        rows = invert([packed[8 * r : 8 * r + 8, :] for r in range(EDGE)])
        for r in range(EDGE):
            packed[8 * r : 8 * r + 8, :] = rows[r]

        def eliminate(s, _):
            tile = packed[pl.ds(s, EDGE, stride=8), :]
            for part in range(PACK):
                c = s * PACK + part
                inverse = spread(tile, part)
                panel = dot(left_parts(inverse), right_parts(before[c, at:first, :]))
                panel = jnp.where(lanes(panel.shape) // EDGE == level, -inverse, panel)
                below = before[c, first:, :]
                change = dot(left_parts(spread(below, level)), right_parts(panel))
                after[c, first:, :] = jnp.where(lanes(below.shape) // EDGE == level, 0.0, below) - change
            return 0

        lax.fori_loop(0, GROUPS // PACK, eliminate, 0, unroll=2)

    def apply(source, _):
        for half in range(ROWS // GROUP):
            c = source * (ROWS // GROUP) + half
            first = half * GROUP
            k = kv_ref[source, first : first + GROUP, :]
            v = kv_ref[source, ROWS + first : ROWS + first + GROUP, :]
            high, low = two_parts(work_even[c, DK:, :])
            vk_high, vk_low = two_parts(vk_start[c])
            mixed = dot(jnp.concatenate([high, high], axis=1), jnp.concatenate([vk_high, vk_low], axis=0))
            mixed = mixed + dot(low, vk_high)
            scores = lax.dot_general(
                jnp.concatenate([high, low], axis=1),
                jnp.concatenate([k, k], axis=1),
                (((1,), (1,)), ((), ())),
                preferred_element_type=f32,
            )
            causal = lanes((GROUP, GROUP)) <= lax.broadcasted_iota(jnp.int32, (GROUP, GROUP), 0)
            high, low = two_parts(jnp.where(causal, scores, 0.0))
            mixed = mixed + dot(high, v) + dot(low, v)
            out_ref[source, first : first + GROUP, :] = mixed.astype(bf16)
        return 0

    lax.fori_loop(0, SOURCES, apply, 0, unroll=2)


def whole():
    return pl.BlockSpec(memory_space=pltpu.VMEM)


def body(queries, key_rows, value_rows, ridge_diag):
    seq = lax.axis_size("seq")
    kv = pl.pallas_call(
        unit_kv_kernel,
        out_shape=jax.ShapeDtypeStruct((HEADS, 2 * ROWS, DK), bf16),
        in_specs=[whole()] * 2,
        out_specs=whole(),
        compiler_params=pltpu.CompilerParams(vmem_limit_bytes=6 * 2**20),
        name="unit_kv",
    )(key_rows, value_rows)
    kv = lax.all_to_all(kv, "head", split_axis=0, concat_axis=0, tiled=True)
    q = pl.pallas_call(
        unit_q_kernel,
        out_shape=jax.ShapeDtypeStruct((HEADS, ROWS, DK), bf16),
        in_specs=[whole()],
        out_specs=whole(),
        compiler_params=pltpu.CompilerParams(vmem_limit_bytes=6 * 2**20),
        name="unit_q",
    )(queries)
    q = lax.all_to_all(q, "head", split_axis=0, concat_axis=0, tiled=True)
    total = pl.pallas_call(
        total_kernel,
        out_shape=jax.ShapeDtypeStruct((DK, 2 * DK), f32),
        in_specs=[whole()],
        out_specs=whole(),
        compiler_params=pltpu.CompilerParams(vmem_limit_bytes=6 * 2**20),
        name="total",
    )(kv)
    partner = lax.ppermute(total, "seq", [(i, i ^ 1) for i in range(seq)])
    chip = total + partner
    earlier = [
        lax.ppermute(chip, "seq", [(i, i + step) for i in range(seq - step)]) for step in range(2, seq, 2)
    ]
    ridge_here = lax.dynamic_slice_in_dim(ridge_diag, lax.axis_index("head"), 1, 0)
    odd = (lax.axis_index("seq") % 2).astype(jnp.int32).reshape(1)
    mixed = pl.pallas_call(
        solve_kernel,
        out_shape=jax.ShapeDtypeStruct((SOURCES, ROWS, DK), bf16),
        in_specs=[pl.BlockSpec(memory_space=pltpu.SMEM)] + [whole()] * 7,
        out_specs=whole(),
        scratch_shapes=[
            pltpu.VMEM((GROUPS + 1, DK + GROUP, DK), f32),
            pltpu.VMEM((GROUPS, DK + GROUP, DK), f32),
            pltpu.VMEM((GROUPS + 1, DK, DK), f32),
            pltpu.VMEM((EDGE * 8, DK), f32),
        ],
        compiler_params=pltpu.CompilerParams(vmem_limit_bytes=16 * 2**20),
        name="solve",
    )(odd, q, kv, *earlier, partner, ridge_here)
    mixed = lax.all_to_all(mixed, "head", split_axis=0, concat_axis=0, tiled=True)
    return pl.pallas_call(
        token_kernel,
        out_shape=jax.ShapeDtypeStruct((ROWS, HEADS * DK), bf16),
        in_specs=[whole()],
        out_specs=whole(),
        compiler_params=pltpu.CompilerParams(vmem_limit_bytes=6 * 2**20),
        name="to_tokens",
    )(mixed)


def solution(mesh):
    in_specs = (P(("seq", "head"), None), P(("seq", "head"), None), P(("seq", "head"), None), P())
    out_specs = P(("seq", "head"), None)
    return jax.shard_map(body, mesh=mesh, in_specs=in_specs, out_specs=out_specs, check_vma=False)
```

```python
import jax
import jax.numpy as jnp
from jax import lax
from jax.experimental import pallas as pl
from jax.experimental.pallas import tpu as pltpu
from jax.sharding import PartitionSpec as P

HEADS = 16
DK = 128
GROUP = 64
ROWS = 128
SOURCES = 16
GROUPS = SOURCES * ROWS // GROUP
EDGE = 32
UNROLL = 2
LEVELS = DK // EDGE
PACK = DK // EDGE

f32, bf16 = jnp.float32, jnp.bfloat16
epsilon = 1e-06


def lanes(shape):
    return lax.broadcasted_iota(jnp.int32, shape, len(shape) - 1)


CHUNKS = 4


def unit_rows(values):
    values_f = values.astype(f32)
    scale_back = lax.rsqrt(jnp.sum(values_f * values_f, axis=-1, keepdims=True) + epsilon)
    return (values_f * scale_back).astype(bf16)


def unit_kernel(q_hbm, k_hbm, v_hbm, out_hbm, taken, ready, in_sems, out_sems):
    rows = ROWS // CHUNKS
    heads = HEADS // CHUNKS
    reads, writes = [], []
    for i, operand in enumerate((q_hbm, k_hbm, v_hbm)):
        for part in range(CHUNKS):
            piece = pl.ds(part * rows, rows)
            reads.append(pltpu.make_async_copy(operand.at[piece], taken.at[i, piece], in_sems.at[i, part]))
            reads[-1].start()
    for i in range(3):
        for part in range(CHUNKS):
            reads[i * CHUNKS + part].wait()
        for part in range(CHUNKS):
            for h in range(part * heads, (part + 1) * heads):
                values = taken[i, :, h * DK : (h + 1) * DK]
                ready[h, i] = values if i == 2 else unit_rows(values)
            piece = pl.ds(part * heads, heads)
            writes.append(pltpu.make_async_copy(ready.at[piece, i], out_hbm.at[piece, i], out_sems.at[i, part]))
            writes[-1].start()
    for write in writes:
        write.wait()


def total_kernel(qkv_ref, out_ref):
    def add(source, total):
        k = qkv_ref[source, ROWS : 2 * ROWS, :]
        v = qkv_ref[source, 2 * ROWS :, :]
        return total + turned_dot(k, jnp.concatenate([k, v], axis=1))

    out_ref[...] = lax.fori_loop(0, SOURCES, add, jnp.zeros((DK, 2 * DK), f32), unroll=True)


def token_kernel(mixed_ref, out_ref):
    for h in range(HEADS):
        out_ref[:, h * DK : (h + 1) * DK] = mixed_ref[h]


def turned_dot(left, right):
    return lax.dot_general(left, right, (((0,), (0,)), ((), ())), preferred_element_type=f32)


def dot(left, right):
    return jnp.dot(left, right, preferred_element_type=f32)


def spread(x, quarter):
    return jnp.take_along_axis(x, quarter * EDGE + lanes(x.shape) % EDGE, axis=1)


def left_parts(x):
    lane = lanes(x.shape)
    rest = x - x.astype(bf16).astype(f32)
    low = rest - rest.astype(bf16).astype(f32)
    first = jnp.where(lane < 3 * EDGE, x, rest).astype(bf16)
    second = jnp.where(lane < EDGE, rest, low).astype(bf16)
    return jnp.concatenate([first, second[:, : 2 * EDGE]], axis=1)


def right_parts(x):
    high = x.astype(bf16)
    rest = x - high.astype(f32)
    middle = rest.astype(bf16)
    low = (rest - middle.astype(f32)).astype(bf16)
    return jnp.concatenate([high, middle, low, high, middle, high], axis=0)


def two_parts(x):
    high = x.astype(bf16)
    return high, (x - high.astype(f32)).astype(bf16)


def invert(rows):
    lane = lanes((8, DK)) % EDGE
    base = lanes((8, DK)) - lane

    def pick(x, j):
        return jnp.take_along_axis(x, base + j, axis=1)

    for j in range(0, EDGE, 2):
        first, second = rows[j], rows[j + 1]
        a, b, d = pick(first, j), pick(first, j + 1), pick(second, j + 1)
        scale = 1.0 / (a * d - b * b)
        a, b, d = a * scale, b * scale, d * scale
        at_first, at_second = lane == j, lane == j + 1
        pivot_first = jnp.where(at_first, d, jnp.where(at_second, -b, d * first - b * second))
        pivot_second = jnp.where(at_first, -b, jnp.where(at_second, a, a * second - b * first))
        for r in [*range(j + 2, EDGE), *range(j)]:
            x = rows[r]
            kept = jnp.where(at_first | at_second, 0.0, x)
            rows[r] = kept - pick(x, j) * pivot_first - pick(x, j + 1) * pivot_second
        rows[j], rows[j + 1] = pivot_first, pivot_second
    return rows


def local_kernel(qkv_ref, gram_ref, vk_ref):
    gram_ref[0] = jnp.zeros((DK, DK), f32)
    vk_ref[0] = jnp.zeros((DK, DK), f32)
    per_source = ROWS // GROUP

    def add(c):
        source = c // per_source
        first = (c % per_source) * GROUP
        k = qkv_ref[source, ROWS + first : ROWS + first + GROUP, :]
        v = qkv_ref[source, 2 * ROWS + first : 2 * ROWS + first + GROUP, :]
        group = turned_dot(k, jnp.concatenate([k, v], axis=1))
        gram_ref[c + 1] = gram_ref[c] + group[:, :DK]
        vk_ref[c + 1] = vk_ref[c] + group[:, DK:]

    for c in range(GROUPS - 1):
        add(c)


def solve_kernel(
    seq_ref, qkv_ref, gram_ref, vk_ref, one_ref, two_ref, three_ref, partner_ref, ridge_ref, out_ref, work_even, work_odd, gram_start, vk_start, packed, panels
):
    row = lax.broadcasted_iota(jnp.int32, (DK, DK), 0)
    diagonal = jnp.where(row == lanes((DK, DK)), jnp.broadcast_to(ridge_ref[...], (DK, DK)), 0.0)
    seq = seq_ref[0]
    start = jnp.where(seq % 2 == 1, partner_ref[...], 0.0)
    for step, ref in enumerate((one_ref, two_ref, three_ref), 1):
        start = start + jnp.where(seq // 2 >= step, ref[...], 0.0)
    gram_start[...] = start[:, :DK] + diagonal
    vk_start[...] = start[:, DK:]

    per_source = ROWS // GROUP
    work = (work_even, work_odd)
    for level in range(LEVELS):
        before, after = work[level % 2], work[1 - level % 2]
        at = level * EDGE
        first = at + EDGE

        def pivot_rows(c):
            if level == 0:
                return gram_ref[c, at:first, :] + gram_start[at:first, :]
            return before[c, at:first, :]

        def rows_below(s, part):
            c = s * PACK + part
            if level > 0:
                return before[c, first:, :]
            source = s * (PACK // per_source) + part // per_source
            token = (part % per_source) * GROUP
            q = qkv_ref[source, token : token + GROUP, :].astype(f32)
            return jnp.concatenate([gram_ref[c, first:, :] + gram_start[first:, :], q], axis=0)

        for s in range(GROUPS // PACK):
            tile = None
            for part in range(PACK):
                block = pivot_rows(s * PACK + part)
                if part != level:
                    block = pltpu.roll(block, (EDGE * (part - level)) % DK, 1)
                tile = block if part == 0 else jnp.where(lanes(block.shape) // EDGE == part, block, tile)
            packed[pl.ds(s, EDGE, stride=8), :] = tile
        rows = invert([packed[8 * r : 8 * r + 8, :] for r in range(EDGE)])
        for r in range(EDGE):
            packed[8 * r : 8 * r + 8, :] = rows[r]

        def scale(s, _):
            tile = packed[pl.ds(s, EDGE, stride=8), :]
            for part in range(PACK):
                c = s * PACK + part
                inverse = spread(tile, part)
                panel = dot(left_parts(inverse), right_parts(pivot_rows(c)))
                panels[c] = right_parts(jnp.where(lanes(panel.shape) // EDGE == level, -inverse, panel))
            return 0

        def eliminate(s, _):
            for part in range(PACK):
                c = s * PACK + part
                below = rows_below(s, part)
                change = dot(left_parts(spread(below, level)), panels[c])
                after[c, first:, :] = jnp.where(lanes(below.shape) // EDGE == level, 0.0, below) - change
            return 0

        lax.fori_loop(0, GROUPS // PACK, scale, 0, unroll=UNROLL)
        lax.fori_loop(0, GROUPS // PACK, eliminate, 0, unroll=UNROLL)

    def apply(source, _):
        for half in range(per_source):
            c = source * per_source + half
            first = half * GROUP
            k = qkv_ref[source, ROWS + first : ROWS + first + GROUP, :]
            v = qkv_ref[source, 2 * ROWS + first : 2 * ROWS + first + GROUP, :]
            high, low = two_parts(work_even[c, DK:, :])
            vk_high, vk_low = two_parts(vk_ref[c] + vk_start[...])
            kk = jnp.concatenate([k, k], axis=1)
            scores = lax.dot_general(
                jnp.concatenate([high, low], axis=1),
                jnp.concatenate([kk, kk], axis=0),
                (((1,), (1,)), ((), ())),
                preferred_element_type=f32,
            )
            lane = lanes((GROUP, 2 * GROUP))
            causal = lane % GROUP <= lax.broadcasted_iota(jnp.int32, (GROUP, 2 * GROUP), 0)
            scores = jnp.where(causal, scores, 0.0)
            rest = scores - scores.astype(bf16).astype(f32)
            scores = jnp.where(lane < GROUP, scores, rest).astype(bf16)
            mixed = dot(
                jnp.concatenate([high, high, low, scores], axis=1),
                jnp.concatenate([vk_high, vk_low, vk_high, v, v], axis=0),
            )
            out_ref[source, first : first + GROUP, :] = mixed.astype(bf16)
        return 0

    lax.fori_loop(0, SOURCES, apply, 0, unroll=2)


def whole():
    return pl.BlockSpec(memory_space=pltpu.VMEM)


def body(queries, key_rows, value_rows, ridge_diag):
    seq = lax.axis_size("seq")
    qkv = pl.pallas_call(
        unit_kernel,
        out_shape=jax.ShapeDtypeStruct((HEADS, 3, ROWS, DK), bf16),
        in_specs=[pl.BlockSpec(memory_space=pl.ANY)] * 3,
        out_specs=pl.BlockSpec(memory_space=pl.ANY),
        scratch_shapes=[
            pltpu.VMEM((3, ROWS, HEADS * DK), bf16),
            pltpu.VMEM((HEADS, 3, ROWS, DK), bf16),
            pltpu.SemaphoreType.DMA((3, CHUNKS)),
            pltpu.SemaphoreType.DMA((3, CHUNKS)),
        ],
        name="unit",
    )(queries, key_rows, value_rows)
    qkv = qkv.reshape(HEADS, 3 * ROWS, DK)
    qkv = lax.all_to_all(qkv, "head", split_axis=0, concat_axis=0, tiled=True)
    total = pl.pallas_call(
        total_kernel,
        out_shape=jax.ShapeDtypeStruct((DK, 2 * DK), f32),
        in_specs=[whole()],
        out_specs=whole(),
        compiler_params=pltpu.CompilerParams(vmem_limit_bytes=6 * 2**20),
        name="total",
    )(qkv)
    partner = lax.ppermute(total, "seq", [(i, i ^ 1) for i in range(seq)])
    chip = total + partner
    earlier = [
        lax.ppermute(chip, "seq", [(i, (i + step) % seq) for i in range(seq)]) for step in range(2, seq, 2)
    ]
    grams, vks = pl.pallas_call(
        local_kernel,
        out_shape=[jax.ShapeDtypeStruct((GROUPS, DK, DK), f32)] * 2,
        in_specs=[whole()],
        out_specs=[whole()] * 2,
        cost_estimate=pl.CostEstimate(flops=2 * 2048 * 128 * 256, bytes_accessed=5 * 2**20, transcendentals=0),
        compiler_params=pltpu.CompilerParams(vmem_limit_bytes=8 * 2**20),
        name="local",
    )(qkv)
    ridge_here = lax.dynamic_slice_in_dim(ridge_diag, lax.axis_index("head"), 1, 0)
    where = lax.axis_index("seq").astype(jnp.int32).reshape(1)
    mixed = pl.pallas_call(
        solve_kernel,
        out_shape=jax.ShapeDtypeStruct((SOURCES, ROWS, DK), bf16),
        in_specs=[pl.BlockSpec(memory_space=pltpu.SMEM)] + [whole()] * 8,
        out_specs=whole(),
        scratch_shapes=[
            pltpu.VMEM((GROUPS, DK + GROUP, DK), f32),
            pltpu.VMEM((GROUPS, DK + GROUP, DK), f32),
            pltpu.VMEM((DK, DK), f32),
            pltpu.VMEM((DK, DK), f32),
            pltpu.VMEM((EDGE * 8, DK), f32),
            pltpu.VMEM((GROUPS, 6 * EDGE, DK), bf16),
        ],
        compiler_params=pltpu.CompilerParams(vmem_limit_bytes=16 * 2**20),
        name="solve",
    )(where, qkv, grams, vks, *earlier, partner, ridge_here)
    mixed = lax.all_to_all(mixed, "head", split_axis=0, concat_axis=0, tiled=True)
    return pl.pallas_call(
        token_kernel,
        out_shape=jax.ShapeDtypeStruct((ROWS, HEADS * DK), bf16),
        in_specs=[whole()],
        out_specs=whole(),
        compiler_params=pltpu.CompilerParams(vmem_limit_bytes=6 * 2**20),
        name="to_tokens",
    )(mixed)


def solution(mesh):
    in_specs = (P(("seq", "head"), None), P(("seq", "head"), None), P(("seq", "head"), None), P())
    out_specs = P(("seq", "head"), None)
    return jax.shard_map(body, mesh=mesh, in_specs=in_specs, out_specs=out_specs, check_vma=False)
```

```python
import jax
import jax.numpy as jnp
from jax import lax
from jax.experimental import pallas as pl
from jax.experimental.pallas import tpu as pltpu
from jax.sharding import PartitionSpec as P

HEADS = 16
DK = 128
GROUP = 64
ROWS = 128
SOURCES = 16
GROUPS = SOURCES * ROWS // GROUP
EDGE = 32
LEVELS = DK // EDGE
PACK = DK // EDGE

f32, bf16 = jnp.float32, jnp.bfloat16
epsilon = 1e-06


def lanes(shape):
    return lax.broadcasted_iota(jnp.int32, shape, len(shape) - 1)


CHUNKS = 4


def unit_rows(values):
    values_f = values.astype(f32)
    scale_back = lax.rsqrt(jnp.sum(values_f * values_f, axis=-1, keepdims=True) + epsilon)
    return (values_f * scale_back).astype(bf16)


def unit_kernel(q_hbm, k_hbm, v_hbm, out_hbm, taken, ready, in_sems, out_sems):
    rows = ROWS // CHUNKS
    heads = HEADS // CHUNKS
    reads, writes = [], []
    for i, operand in enumerate((q_hbm, k_hbm, v_hbm)):
        for part in range(CHUNKS):
            piece = pl.ds(part * rows, rows)
            reads.append(pltpu.make_async_copy(operand.at[piece], taken.at[i, piece], in_sems.at[i, part]))
            reads[-1].start()
    for i in range(3):
        for part in range(CHUNKS):
            reads[i * CHUNKS + part].wait()
        for part in range(CHUNKS):
            for h in range(part * heads, (part + 1) * heads):
                values = taken[i, :, h * DK : (h + 1) * DK]
                ready[h, i] = values if i == 2 else unit_rows(values)
            piece = pl.ds(part * heads, heads)
            writes.append(pltpu.make_async_copy(ready.at[piece, i], out_hbm.at[piece, i], out_sems.at[i, part]))
            writes[-1].start()
    for write in writes:
        write.wait()


def total_kernel(qkv_ref, out_ref):
    def add(source, total):
        k = qkv_ref[source, ROWS : 2 * ROWS, :]
        v = qkv_ref[source, 2 * ROWS :, :]
        return total + turned_dot(k, jnp.concatenate([k, v], axis=1))

    out_ref[...] = lax.fori_loop(0, SOURCES, add, jnp.zeros((DK, 2 * DK), f32), unroll=True)


def token_kernel(mixed_hbm, out_hbm, sems):
    copies = [
        pltpu.make_async_copy(mixed_hbm.at[h], out_hbm.at[:, pl.ds(h * DK, DK)], sems.at[h]) for h in range(HEADS)
    ]
    for copy in copies:
        copy.start()
    for copy in copies:
        copy.wait()


def turned_dot(left, right):
    return lax.dot_general(left, right, (((0,), (0,)), ((), ())), preferred_element_type=f32)


def dot(left, right):
    return jnp.dot(left, right, preferred_element_type=f32)


def spread(x, quarter):
    return jnp.take_along_axis(x, quarter * EDGE + lanes(x.shape) % EDGE, axis=1)


def left_parts(x):
    lane = lanes(x.shape)
    rest = x - x.astype(bf16).astype(f32)
    low = rest - rest.astype(bf16).astype(f32)
    first = jnp.where(lane < 3 * EDGE, x, rest).astype(bf16)
    second = jnp.where(lane < EDGE, rest, low).astype(bf16)
    return jnp.concatenate([first, second[:, : 2 * EDGE]], axis=1)


def right_parts(x):
    high = x.astype(bf16)
    rest = x - high.astype(f32)
    middle = rest.astype(bf16)
    low = (rest - middle.astype(f32)).astype(bf16)
    return jnp.concatenate([high, middle, low, high, middle, high], axis=0)


def two_parts(x):
    high = x.astype(bf16)
    return high, (x - high.astype(f32)).astype(bf16)


def invert(rows):
    lane = lanes((8, DK)) % EDGE
    base = lanes((8, DK)) - lane

    def pick(x, j):
        return jnp.take_along_axis(x, base + j, axis=1)

    for j in range(0, EDGE, 2):
        first, second = rows[j], rows[j + 1]
        a, b, d = pick(first, j), pick(first, j + 1), pick(second, j + 1)
        scale = 1.0 / (a * d - b * b)
        a, b, d = a * scale, b * scale, d * scale
        at_first, at_second = lane == j, lane == j + 1
        pivot_first = jnp.where(at_first, d, jnp.where(at_second, -b, d * first - b * second))
        pivot_second = jnp.where(at_first, -b, jnp.where(at_second, a, a * second - b * first))
        for r in [*range(j + 2, EDGE), *range(j)]:
            x = rows[r]
            kept = jnp.where(at_first | at_second, 0.0, x)
            rows[r] = kept - pick(x, j) * pivot_first - pick(x, j + 1) * pivot_second
        rows[j], rows[j + 1] = pivot_first, pivot_second
    return rows


def local_kernel(qkv_ref, gram_ref, vk_ref):
    gram_ref[0] = jnp.zeros((DK, DK), f32)
    vk_ref[0] = jnp.zeros((DK, DK), f32)
    per_source = ROWS // GROUP

    def add(c):
        source = c // per_source
        first = (c % per_source) * GROUP
        k = qkv_ref[source, ROWS + first : ROWS + first + GROUP, :]
        v = qkv_ref[source, 2 * ROWS + first : 2 * ROWS + first + GROUP, :]
        group = turned_dot(k, jnp.concatenate([k, v], axis=1))
        gram_ref[c + 1] = gram_ref[c] + group[:, :DK]
        vk_ref[c + 1] = vk_ref[c] + group[:, DK:]

    for c in range(GROUPS - 1):
        add(c)


def solve_kernel(
    seq_ref, qkv_ref, gram_ref, vk_ref, one_ref, two_ref, three_ref, partner_ref, ridge_ref, out_ref, work_even, work_odd, gram_start, vk_start, packed, panels
):
    row = lax.broadcasted_iota(jnp.int32, (DK, DK), 0)
    diagonal = jnp.where(row == lanes((DK, DK)), jnp.broadcast_to(ridge_ref[...], (DK, DK)), 0.0)
    seq = seq_ref[0]
    start = jnp.where(seq % 2 == 1, partner_ref[...], 0.0)
    for step, ref in enumerate((one_ref, two_ref, three_ref), 1):
        start = start + jnp.where(seq // 2 >= step, ref[...], 0.0)
    gram_start[...] = start[:, :DK] + diagonal
    vk_start[...] = start[:, DK:]

    per_source = ROWS // GROUP
    work = (work_even, work_odd)
    for level in range(LEVELS):
        before, after = work[level % 2], work[1 - level % 2]
        at = level * EDGE
        first = at + EDGE

        def pivot_rows(c):
            if level == 0:
                return gram_ref[c, at:first, :] + gram_start[at:first, :]
            return before[c, at:first, :]

        def rows_below(s, part):
            c = s * PACK + part
            if level > 0:
                return before[c, first:, :]
            source = s * (PACK // per_source) + part // per_source
            token = (part % per_source) * GROUP
            q = qkv_ref[source, token : token + GROUP, :].astype(f32)
            return jnp.concatenate([gram_ref[c, first:, :] + gram_start[first:, :], q], axis=0)

        for s in range(GROUPS // PACK):
            tile = None
            for part in range(PACK):
                block = pivot_rows(s * PACK + part)
                if part != level:
                    block = pltpu.roll(block, (EDGE * (part - level)) % DK, 1)
                tile = block if part == 0 else jnp.where(lanes(block.shape) // EDGE == part, block, tile)
            packed[pl.ds(s, EDGE, stride=8), :] = tile
        rows = invert([packed[8 * r : 8 * r + 8, :] for r in range(EDGE)])
        for r in range(EDGE):
            packed[8 * r : 8 * r + 8, :] = rows[r]

        def scale(s, _):
            tile = packed[pl.ds(s, EDGE, stride=8), :]
            for part in range(PACK):
                c = s * PACK + part
                inverse = spread(tile, part)
                panel = dot(left_parts(inverse), right_parts(pivot_rows(c)))
                panels[c] = right_parts(jnp.where(lanes(panel.shape) // EDGE == level, -inverse, panel))
            return 0

        def eliminate(s, _):
            for part in range(PACK):
                c = s * PACK + part
                below = rows_below(s, part)
                change = dot(left_parts(spread(below, level)), panels[c])
                after[c, first:, :] = jnp.where(lanes(below.shape) // EDGE == level, 0.0, below) - change
            return 0

        lax.fori_loop(0, GROUPS // PACK, scale, 0, unroll=True)
        lax.fori_loop(0, GROUPS // PACK, eliminate, 0, unroll=True)

    def apply(source, _):
        for half in range(per_source):
            c = source * per_source + half
            first = half * GROUP
            k = qkv_ref[source, ROWS + first : ROWS + first + GROUP, :]
            v = qkv_ref[source, 2 * ROWS + first : 2 * ROWS + first + GROUP, :]
            high, low = two_parts(work_even[c, DK:, :])
            vk_high, vk_low = two_parts(vk_ref[c] + vk_start[...])
            kk = jnp.concatenate([k, k], axis=1)
            scores = lax.dot_general(
                jnp.concatenate([high, low], axis=1),
                jnp.concatenate([kk, kk], axis=0),
                (((1,), (1,)), ((), ())),
                preferred_element_type=f32,
            )
            lane = lanes((GROUP, 2 * GROUP))
            causal = lane % GROUP <= lax.broadcasted_iota(jnp.int32, (GROUP, 2 * GROUP), 0)
            scores = jnp.where(causal, scores, 0.0)
            rest = scores - scores.astype(bf16).astype(f32)
            scores = jnp.where(lane < GROUP, scores, rest).astype(bf16)
            mixed = dot(
                jnp.concatenate([high, high, low, scores], axis=1),
                jnp.concatenate([vk_high, vk_low, vk_high, v, v], axis=0),
            )
            out_ref[source, first : first + GROUP, :] = mixed.astype(bf16)
        return 0

    lax.fori_loop(0, SOURCES, apply, 0, unroll=True)


def whole():
    return pl.BlockSpec(memory_space=pltpu.VMEM)


def body(queries, key_rows, value_rows, ridge_diag):
    seq = lax.axis_size("seq")
    qkv = pl.pallas_call(
        unit_kernel,
        out_shape=jax.ShapeDtypeStruct((HEADS, 3, ROWS, DK), bf16),
        in_specs=[pl.BlockSpec(memory_space=pl.ANY)] * 3,
        out_specs=pl.BlockSpec(memory_space=pl.ANY),
        scratch_shapes=[
            pltpu.VMEM((3, ROWS, HEADS * DK), bf16),
            pltpu.VMEM((HEADS, 3, ROWS, DK), bf16),
            pltpu.SemaphoreType.DMA((3, CHUNKS)),
            pltpu.SemaphoreType.DMA((3, CHUNKS)),
        ],
        name="unit",
    )(queries, key_rows, value_rows)
    qkv = qkv.reshape(HEADS, 3 * ROWS, DK)
    qkv = lax.all_to_all(qkv, "head", split_axis=0, concat_axis=0, tiled=True)
    total = pl.pallas_call(
        total_kernel,
        out_shape=jax.ShapeDtypeStruct((DK, 2 * DK), f32),
        in_specs=[whole()],
        out_specs=whole(),
        compiler_params=pltpu.CompilerParams(vmem_limit_bytes=6 * 2**20),
        name="total",
    )(qkv)
    partner = lax.ppermute(total, "seq", [(i, i ^ 1) for i in range(seq)])
    chip = total + partner
    earlier = [
        lax.ppermute(chip, "seq", [(i, (i + step) % seq) for i in range(seq)]) for step in range(2, seq, 2)
    ]
    grams, vks = pl.pallas_call(
        local_kernel,
        out_shape=[jax.ShapeDtypeStruct((GROUPS, DK, DK), f32)] * 2,
        in_specs=[whole()],
        out_specs=[whole()] * 2,
        cost_estimate=pl.CostEstimate(flops=2 * 2048 * 128 * 256, bytes_accessed=5 * 2**20, transcendentals=0),
        compiler_params=pltpu.CompilerParams(vmem_limit_bytes=8 * 2**20),
        name="local",
    )(qkv)
    ridge_here = lax.dynamic_slice_in_dim(ridge_diag, lax.axis_index("head"), 1, 0)
    where = lax.axis_index("seq").astype(jnp.int32).reshape(1)
    mixed = pl.pallas_call(
        solve_kernel,
        out_shape=jax.ShapeDtypeStruct((SOURCES, ROWS, DK), bf16),
        in_specs=[pl.BlockSpec(memory_space=pltpu.SMEM)] + [whole()] * 8,
        out_specs=whole(),
        scratch_shapes=[
            pltpu.VMEM((GROUPS, DK + GROUP, DK), f32),
            pltpu.VMEM((GROUPS, DK + GROUP, DK), f32),
            pltpu.VMEM((DK, DK), f32),
            pltpu.VMEM((DK, DK), f32),
            pltpu.VMEM((EDGE * 8, DK), f32),
            pltpu.VMEM((GROUPS, 6 * EDGE, DK), bf16),
        ],
        compiler_params=pltpu.CompilerParams(vmem_limit_bytes=16 * 2**20),
        name="solve",
    )(where, qkv, grams, vks, *earlier, partner, ridge_here)
    mixed = lax.all_to_all(mixed, "head", split_axis=0, concat_axis=0, tiled=True)
    return pl.pallas_call(
        token_kernel,
        out_shape=jax.ShapeDtypeStruct((ROWS, HEADS * DK), bf16),
        in_specs=[pl.BlockSpec(memory_space=pl.ANY)],
        out_specs=pl.BlockSpec(memory_space=pl.ANY),
        scratch_shapes=[pltpu.SemaphoreType.DMA((HEADS,))],
        compiler_params=pltpu.CompilerParams(vmem_limit_bytes=4 * 2**20),
        name="to_tokens",
    )(mixed)


def solution(mesh):
    in_specs = (P(("seq", "head"), None), P(("seq", "head"), None), P(("seq", "head"), None), P())
    out_specs = P(("seq", "head"), None)
    return jax.shard_map(body, mesh=mesh, in_specs=in_specs, out_specs=out_specs, check_vma=False)
```

```python
import jax
import jax.numpy as jnp
from jax import lax
from jax.experimental import pallas as pl
from jax.experimental.pallas import tpu as pltpu
from jax.sharding import PartitionSpec as P

HEADS = 16
DK = 128
GROUP = 64
ROWS = 128
SOURCES = 16
GROUPS = SOURCES * ROWS // GROUP
EDGE = 32
LEVELS = DK // EDGE
PACK = DK // EDGE

f32, bf16 = jnp.float32, jnp.bfloat16
epsilon = 1e-06


def lanes(shape):
    return lax.broadcasted_iota(jnp.int32, shape, len(shape) - 1)


CHUNKS = 4


def unit_rows(values):
    values_f = values.astype(f32)
    scale_back = lax.rsqrt(jnp.sum(values_f * values_f, axis=-1, keepdims=True) + epsilon)
    return (values_f * scale_back).astype(bf16)


def unit_kernel(q_hbm, k_hbm, v_hbm, out_hbm, taken, ready, in_sems, out_sems):
    rows = ROWS // CHUNKS
    heads = HEADS // CHUNKS
    reads, writes = [], []
    for i, operand in enumerate((q_hbm, k_hbm, v_hbm)):
        for part in range(CHUNKS):
            piece = pl.ds(part * rows, rows)
            reads.append(pltpu.make_async_copy(operand.at[piece], taken.at[i, piece], in_sems.at[i, part]))
            reads[-1].start()
    for i in range(3):
        for part in range(CHUNKS):
            reads[i * CHUNKS + part].wait()
        for part in range(CHUNKS):
            for h in range(part * heads, (part + 1) * heads):
                values = taken[i, :, h * DK : (h + 1) * DK]
                ready[h, i] = values if i == 2 else unit_rows(values)
            piece = pl.ds(part * heads, heads)
            writes.append(pltpu.make_async_copy(ready.at[piece, i], out_hbm.at[piece, i], out_sems.at[i, part]))
            writes[-1].start()
    for write in writes:
        write.wait()


def total_kernel(qkv_ref, out_ref):
    def add(source, total):
        k = qkv_ref[source, ROWS : 2 * ROWS, :]
        v = qkv_ref[source, 2 * ROWS :, :]
        return total + turned_dot(k, jnp.concatenate([k, v], axis=1))

    total = lax.fori_loop(0, SOURCES, add, jnp.zeros((DK, 2 * DK), f32), unroll=True)
    out_ref[:DK, :] = total[:, :DK]
    out_ref[DK:, :] = total[:, DK:]


def token_kernel(mixed_hbm, out_hbm, sems):
    copies = [
        pltpu.make_async_copy(mixed_hbm.at[h], out_hbm.at[:, pl.ds(h * DK, DK)], sems.at[h]) for h in range(HEADS)
    ]
    for copy in copies:
        copy.start()
    for copy in copies:
        copy.wait()


def turned_dot(left, right):
    return lax.dot_general(left, right, (((0,), (0,)), ((), ())), preferred_element_type=f32)


def dot(left, right):
    return jnp.dot(left, right, preferred_element_type=f32)


def spread(x, quarter):
    return jnp.take_along_axis(x, quarter * EDGE + lanes(x.shape) % EDGE, axis=1)


def left_parts(x):
    lane = lanes(x.shape)
    rest = x - x.astype(bf16).astype(f32)
    low = rest - rest.astype(bf16).astype(f32)
    first = jnp.where(lane < 3 * EDGE, x, rest).astype(bf16)
    second = jnp.where(lane < EDGE, rest, low).astype(bf16)
    return jnp.concatenate([first, second[:, : 2 * EDGE]], axis=1)


def right_parts(x):
    high = x.astype(bf16)
    rest = x - high.astype(f32)
    middle = rest.astype(bf16)
    low = (rest - middle.astype(f32)).astype(bf16)
    return jnp.concatenate([high, middle, low, high, middle, high], axis=0)


def two_parts(x):
    high = x.astype(bf16)
    return high, (x - high.astype(f32)).astype(bf16)


def invert(rows):
    lane = lanes((8, DK)) % EDGE
    base = lanes((8, DK)) - lane

    def pick(x, j):
        return jnp.take_along_axis(x, base + j, axis=1)

    for j in range(0, EDGE, 2):
        first, second = rows[j], rows[j + 1]
        a, b, d = pick(first, j), pick(first, j + 1), pick(second, j + 1)
        scale = 1.0 / (a * d - b * b)
        a, b, d = a * scale, b * scale, d * scale
        at_first, at_second = lane == j, lane == j + 1
        pivot_first = jnp.where(at_first, d, jnp.where(at_second, -b, d * first - b * second))
        pivot_second = jnp.where(at_first, -b, jnp.where(at_second, a, a * second - b * first))
        for r in [*range(j + 2, EDGE), *range(j)]:
            x = rows[r]
            kept = jnp.where(at_first | at_second, 0.0, x)
            rows[r] = kept - pick(x, j) * pivot_first - pick(x, j + 1) * pivot_second
        rows[j], rows[j + 1] = pivot_first, pivot_second
    return rows


def local_kernel(qkv_ref, gram_ref, vk_ref):
    gram_ref[0] = jnp.zeros((DK, DK), f32)
    vk_ref[0] = jnp.zeros((DK, DK), f32)
    per_source = ROWS // GROUP

    def add(c):
        source = c // per_source
        first = (c % per_source) * GROUP
        k = qkv_ref[source, ROWS + first : ROWS + first + GROUP, :]
        v = qkv_ref[source, 2 * ROWS + first : 2 * ROWS + first + GROUP, :]
        group = turned_dot(k, jnp.concatenate([k, v], axis=1))
        gram_ref[c + 1] = gram_ref[c] + group[:, :DK]
        vk_ref[c + 1] = vk_ref[c] + group[:, DK:]

    for c in range(GROUPS - 1):
        add(c)


def earlier_sum(seq, partner, steps):
    start = jnp.where(seq % 2 == 1, partner, 0.0)
    for step, ref in enumerate(steps, 1):
        start = start + jnp.where(seq // 2 >= step, ref[...], 0.0)
    return start


def solve_kernel(
    seq_ref, qkv_ref, gram_ref, one_ref, two_ref, three_ref, partner_ref, ridge_ref, solved_ref, work_even, work_odd, gram_start, packed, panels
):
    row = lax.broadcasted_iota(jnp.int32, (DK, DK), 0)
    diagonal = jnp.where(row == lanes((DK, DK)), jnp.broadcast_to(ridge_ref[...], (DK, DK)), 0.0)
    start = earlier_sum(seq_ref[0], partner_ref[:DK, :], (one_ref, two_ref, three_ref))
    gram_start[...] = start + diagonal

    per_source = ROWS // GROUP
    work = (work_even, work_odd)
    for level in range(LEVELS):
        before, after = work[level % 2], work[1 - level % 2]
        at = level * EDGE
        first = at + EDGE

        def pivot_rows(c):
            if level == 0:
                return gram_ref[c, at:first, :] + gram_start[at:first, :]
            return before[c, at:first, :]

        def rows_below(s, part):
            c = s * PACK + part
            if level > 0:
                return before[c, first:, :]
            source = s * (PACK // per_source) + part // per_source
            token = (part % per_source) * GROUP
            q = qkv_ref[source, token : token + GROUP, :].astype(f32)
            return jnp.concatenate([gram_ref[c, first:, :] + gram_start[first:, :], q], axis=0)

        for s in range(GROUPS // PACK):
            tile = None
            for part in range(PACK):
                block = pivot_rows(s * PACK + part)
                if part != level:
                    block = pltpu.roll(block, (EDGE * (part - level)) % DK, 1)
                tile = block if part == 0 else jnp.where(lanes(block.shape) // EDGE == part, block, tile)
            packed[pl.ds(s, EDGE, stride=8), :] = tile
        rows = invert([packed[8 * r : 8 * r + 8, :] for r in range(EDGE)])
        for r in range(EDGE):
            packed[8 * r : 8 * r + 8, :] = rows[r]

        def scale(s, _):
            tile = packed[pl.ds(s, EDGE, stride=8), :]
            for part in range(PACK):
                c = s * PACK + part
                inverse = spread(tile, part)
                panel = dot(left_parts(inverse), right_parts(pivot_rows(c)))
                panels[c] = right_parts(jnp.where(lanes(panel.shape) // EDGE == level, -inverse, panel))
            return 0

        def eliminate(s, _):
            for part in range(PACK):
                c = s * PACK + part
                below = rows_below(s, part)
                change = dot(left_parts(spread(below, level)), panels[c])
                below = jnp.where(lanes(below.shape) // EDGE == level, 0.0, below) - change
                if level < LEVELS - 1:
                    after[c, first:, :] = below
                else:
                    solved_ref[c] = below
            return 0

        lax.fori_loop(0, GROUPS // PACK, scale, 0, unroll=True)
        lax.fori_loop(0, GROUPS // PACK, eliminate, 0, unroll=True)


def mix_kernel(seq_ref, solved_ref, qkv_ref, vk_ref, one_ref, two_ref, three_ref, partner_ref, out_ref, vk_start):
    vk_start[...] = earlier_sum(seq_ref[0], partner_ref[DK:, :], (one_ref, two_ref, three_ref))
    per_source = ROWS // GROUP

    def apply(source, _):
        for half in range(per_source):
            c = source * per_source + half
            first = half * GROUP
            k = qkv_ref[source, ROWS + first : ROWS + first + GROUP, :]
            v = qkv_ref[source, 2 * ROWS + first : 2 * ROWS + first + GROUP, :]
            high, low = two_parts(solved_ref[c])
            vk_high, vk_low = two_parts(vk_ref[c] + vk_start[...])
            kk = jnp.concatenate([k, k], axis=1)
            scores = lax.dot_general(
                jnp.concatenate([high, low], axis=1),
                jnp.concatenate([kk, kk], axis=0),
                (((1,), (1,)), ((), ())),
                preferred_element_type=f32,
            )
            lane = lanes((GROUP, 2 * GROUP))
            causal = lane % GROUP <= lax.broadcasted_iota(jnp.int32, (GROUP, 2 * GROUP), 0)
            scores = jnp.where(causal, scores, 0.0)
            rest = scores - scores.astype(bf16).astype(f32)
            scores = jnp.where(lane < GROUP, scores, rest).astype(bf16)
            mixed = dot(
                jnp.concatenate([high, high, low, scores], axis=1),
                jnp.concatenate([vk_high, vk_low, vk_high, v, v], axis=0),
            )
            out_ref[source, first : first + GROUP, :] = mixed.astype(bf16)
        return 0

    lax.fori_loop(0, SOURCES, apply, 0, unroll=True)


def whole():
    return pl.BlockSpec(memory_space=pltpu.VMEM)


def body(queries, key_rows, value_rows, ridge_diag):
    seq = lax.axis_size("seq")
    qkv = pl.pallas_call(
        unit_kernel,
        out_shape=jax.ShapeDtypeStruct((HEADS, 3, ROWS, DK), bf16),
        in_specs=[pl.BlockSpec(memory_space=pl.ANY)] * 3,
        out_specs=pl.BlockSpec(memory_space=pl.ANY),
        scratch_shapes=[
            pltpu.VMEM((3, ROWS, HEADS * DK), bf16),
            pltpu.VMEM((HEADS, 3, ROWS, DK), bf16),
            pltpu.SemaphoreType.DMA((3, CHUNKS)),
            pltpu.SemaphoreType.DMA((3, CHUNKS)),
        ],
        name="unit",
    )(queries, key_rows, value_rows)
    qkv = qkv.reshape(HEADS, 3 * ROWS, DK)
    qkv = lax.all_to_all(qkv, "head", split_axis=0, concat_axis=0, tiled=True)
    total = pl.pallas_call(
        total_kernel,
        out_shape=jax.ShapeDtypeStruct((2 * DK, DK), f32),
        in_specs=[whole()],
        out_specs=whole(),
        compiler_params=pltpu.CompilerParams(vmem_limit_bytes=6 * 2**20),
        name="total",
    )(qkv)
    partner = lax.ppermute(total, "seq", [(i, i ^ 1) for i in range(seq)])
    def from_earlier(chip):
        return [
            lax.ppermute(chip, "seq", [(i, (i + step) % seq) for i in range(seq)]) for step in range(2, seq, 2)
        ]

    gram_steps = from_earlier(total[:DK] + partner[:DK])
    vk_steps = from_earlier(total[DK:] + partner[DK:])
    grams, vks = pl.pallas_call(
        local_kernel,
        out_shape=[jax.ShapeDtypeStruct((GROUPS, DK, DK), f32)] * 2,
        in_specs=[whole()],
        out_specs=[whole()] * 2,
        cost_estimate=pl.CostEstimate(flops=2 * 2048 * 128 * 256, bytes_accessed=5 * 2**20, transcendentals=0),
        compiler_params=pltpu.CompilerParams(vmem_limit_bytes=8 * 2**20),
        name="local",
    )(qkv)
    ridge_here = lax.dynamic_slice_in_dim(ridge_diag, lax.axis_index("head"), 1, 0)
    where = lax.axis_index("seq").astype(jnp.int32).reshape(1)
    scalar = pl.BlockSpec(memory_space=pltpu.SMEM)
    solved = pl.pallas_call(
        solve_kernel,
        out_shape=jax.ShapeDtypeStruct((GROUPS, GROUP, DK), f32),
        in_specs=[scalar] + [whole()] * 7,
        out_specs=whole(),
        scratch_shapes=[
            pltpu.VMEM((GROUPS, DK + GROUP, DK), f32),
            pltpu.VMEM((GROUPS, DK + GROUP, DK), f32),
            pltpu.VMEM((DK, DK), f32),
            pltpu.VMEM((EDGE * 8, DK), f32),
            pltpu.VMEM((GROUPS, 6 * EDGE, DK), bf16),
        ],
        cost_estimate=pl.CostEstimate(flops=10**10, bytes_accessed=30 * 2**20, transcendentals=0),
        compiler_params=pltpu.CompilerParams(vmem_limit_bytes=16 * 2**20),
        name="solve",
    )(where, qkv, grams, *gram_steps, partner, ridge_here)
    mixed = pl.pallas_call(
        mix_kernel,
        out_shape=jax.ShapeDtypeStruct((SOURCES, ROWS, DK), bf16),
        in_specs=[scalar] + [whole()] * 7,
        out_specs=whole(),
        scratch_shapes=[pltpu.VMEM((DK, DK), f32)],
        compiler_params=pltpu.CompilerParams(vmem_limit_bytes=8 * 2**20),
        name="mix",
    )(where, solved, qkv, vks, *vk_steps, partner)
    mixed = lax.all_to_all(mixed, "head", split_axis=0, concat_axis=0, tiled=True)
    return pl.pallas_call(
        token_kernel,
        out_shape=jax.ShapeDtypeStruct((ROWS, HEADS * DK), bf16),
        in_specs=[pl.BlockSpec(memory_space=pl.ANY)],
        out_specs=pl.BlockSpec(memory_space=pl.ANY),
        scratch_shapes=[pltpu.SemaphoreType.DMA((HEADS,))],
        compiler_params=pltpu.CompilerParams(vmem_limit_bytes=4 * 2**20),
        name="to_tokens",
    )(mixed)


def solution(mesh):
    in_specs = (P(("seq", "head"), None), P(("seq", "head"), None), P(("seq", "head"), None), P())
    out_specs = P(("seq", "head"), None)
    return jax.shard_map(body, mesh=mesh, in_specs=in_specs, out_specs=out_specs, check_vma=False)
```
